32 devices in a mesh: node: 8 (over y, x, core), mode: 4 (over z).
Axes of the slice: x: 2, y: 2, z: 4, core: 2. Of those that a mesh axis runs over, the one named last changes fastest.
Arguments:
- coords: float32 [3, 196608], P(None, 'node'), may hold values from 0 to 4
- wavevec: float32 [3, 256], replicated, may hold values from -6 to 6
- wave_amp: float32 [2, 256], replicated, may hold values from -6 to 6
- mode_shapes: bfloat16 [2000, 196608], P('mode', 'node'), may hold values from -0.013671875 to 0.013671875
- modal_frf: float32 [2, 2000], P(None, 'mode'), may hold values from -6 to 6
- radiation: bfloat16 [2, 2000, 4096], P(None, 'mode', 'node'), may hold values from -0.125 to 0.125
Outputs:
- cross_spectrum: float32 [2, 4096, 4096], P(None, ('node', 'mode'))
- field_pressure: bfloat16 [4096, 512], P(('node', 'mode'))
The draws below stay inside these ranges and needn't reach their ends.
All inputs are finite; a program needn't handle non-finite values.
Results may differ from the reference program's by a relative error of at most 0.0065.
Values may be sent and summed in bfloat16 or wider, within the bound.
No kernel may reach another device: no remote copies, remote signals or barrier semaphores. Data moves between devices by JAX's collectives and lax.ppermute only.
A program may use at most 64 MiB of HBM per device.

```python
import jax
import jax.numpy as jnp
from jax import lax

ND = 24576
MODES = 2000
W = 256
NODES = 196608
FIELD = 4096


def levels(own_key, shape, split, low, high):
    loudness, own = 1.0, jax.random.fold_in(own_key, 6)
    for axis_at, parts in split:
        steps = jnp.exp(jax.random.uniform(jax.random.fold_in(own, axis_at), (parts,), jnp.float32, low / len(split), high / len(split)))
        loudness = loudness * jnp.repeat(steps, shape[axis_at] // parts).reshape([-1 if axis == axis_at else 1 for axis in range(len(shape))])
    return loudness


def scatter_about(key, extent, spread, most, split=(), kind=jnp.bfloat16):
    values = jax.random.normal(key, extent, jnp.float32) * spread
    if len(split) > 0:
        values = levels(key, extent, split, -0.22, 0.18) * values
    return jnp.clip(values, min=-most, max=most).astype(kind)


def setup_inputs(seed: int = 0) -> dict:
    splits = jax.random.split(jax.random.key(seed), 7)
    return {
        "coords": jnp.clip(4.0 * jax.random.uniform(splits[0], (3, NODES), jnp.float32) ** levels(splits[0], (3, NODES), ((1, 8),), -0.2, 0.2), 0.0, 4.0),
        "wavevec": jnp.clip(jax.random.uniform(splits[1], (3, W), jnp.float32, -6.0, 6.0), -6.0, 6.0),
        "wave_amp": scatter_about(splits[2], (2, W), 1.0, 6.0, (), jnp.float32),
        "mode_shapes": scatter_about(splits[3], (MODES, NODES), NODES ** -0.5, 0.013671875, ((0, 4), (1, 8))),
        "modal_frf": scatter_about(splits[4], (2, MODES), 1.0, 6.0, ((1, 4),), jnp.float32),
        "radiation": scatter_about(splits[5], (2, MODES, FIELD), MODES ** -0.5, 0.125, ((1, 4), (2, 8))),
    }


def pressure_block(position, wavevec, wave_amp):
    phases = position[0][:, None] * wavevec[0][None, :] + position[1][:, None] * wavevec[1][None, :] + position[2][:, None] * wavevec[2][None, :]
    cosine = jnp.cos(phases)
    sines = jnp.sin(phases)
    real_part = wave_amp[0][None, :] * cosine - wave_amp[1][None, :] * sines
    imag_part = wave_amp[0][None, :] * sines + wave_amp[1][None, :] * cosine
    return jnp.concatenate([real_part, imag_part], axis=1).astype(jnp.bfloat16)


def modal_forces(coords, wavevec, wave_amp, mode_shapes, stride):
    block_count = mode_shapes.shape[1] // stride

    def advance(summed, number):
        offset = (number * stride).astype(jnp.int32)
        position = lax.dynamic_slice_in_dim(coords, offset, stride, 1)
        shapes = lax.dynamic_slice_in_dim(mode_shapes, offset, stride, 1)
        pressures = pressure_block(position, wavevec, wave_amp)
        product = jnp.dot(shapes, pressures, preferred_element_type=jnp.float32)
        return summed + product, None

    initial = jnp.zeros((mode_shapes.shape[0], 2 * wavevec.shape[1]), jnp.float32)
    summed, _ = lax.scan(advance, initial, jnp.arange(block_count, dtype=jnp.int32))
    return summed


def modal_response(forces, modal_frf):
    waves_count = forces.shape[1] // 2
    force_real = forces[:, :waves_count]
    force_imag = forces[:, waves_count:]
    gain_real = modal_frf[0][:, None]
    gain_imag = modal_frf[1][:, None]
    modal_real = gain_real * force_real - gain_imag * force_imag
    modal_imag = gain_real * force_imag + gain_imag * force_real
    upper = jnp.concatenate([modal_real, modal_imag], axis=1)
    lower = jnp.concatenate([-modal_imag, modal_real], axis=1)
    return jnp.concatenate([upper, lower], axis=0).astype(jnp.bfloat16)


def cross_spectra(owned_rows, others):
    waves_count = owned_rows.shape[1] // 2
    turned = jnp.concatenate([owned_rows[:, waves_count:], -owned_rows[:, :waves_count]], axis=1)
    stacked = jnp.concatenate([owned_rows, turned], axis=0)
    product = lax.dot_general(stacked, others, (((1,), (1,)), ((), ())), preferred_element_type=jnp.float32)
    return product.reshape(2, owned_rows.shape[0], others.shape[0]) * (1.0 / waves_count)


def reference(coords, wavevec, wave_amp, mode_shapes, modal_frf, radiation):
    forces = modal_forces(coords, wavevec, wave_amp, mode_shapes, min(2048, ND))
    operand = modal_response(forces, modal_frf)
    transfer = radiation.reshape(2 * radiation.shape[1], radiation.shape[2])
    summed = lax.dot_general(transfer, operand, (((0,), (0,)), ((), ())), preferred_element_type=jnp.float32)
    field_pressure = summed.astype(jnp.bfloat16)
    return cross_spectra(field_pressure, field_pressure), field_pressure
```

```python
import functools

import jax
import jax.numpy as jnp
from jax import lax
from jax.experimental import pallas as pl
from jax.experimental.pallas import tpu as pltpu
from jax.sharding import PartitionSpec as P

SINE = (4.441535719696892, -7.264680836400963, 3.2520496076552887)
COSINE = (1.414204080330576, -6.977642043687199, 5.715238221214665, -1.7283481089755481)
COORD_PIECES = (0, 0, 1, 1, 0, 2)
WAVE_PIECES = (0, 1, 0, 1, 2, 0)
TURNS = 0.15915494309189535


def circle(turns):
    r = turns - jnp.round(turns)
    u = r * r
    s = r * (SINE[0] + u * (SINE[1] + u * SINE[2]))
    c = COSINE[0] + u * (COSINE[1] + u * (COSINE[2] + u * COSINE[3]))
    return c * c - 1.0, s * c


def pieces(x, order):
    first = x.astype(jnp.bfloat16).astype(jnp.float32)
    second = (x - first).astype(jnp.bfloat16).astype(jnp.float32)
    third = x - first - second
    blank = jnp.zeros((8 - x.shape[0], x.shape[1]), jnp.float32)
    parts = [jnp.concatenate([p, blank], axis=0) for p in (first, second, third)]
    return jnp.concatenate([parts[i] for i in order], axis=0).astype(jnp.bfloat16)


def forces_kernel(half, sub, coords_ref, wave_ref, shapes_ref, out_ref, wave_pieces, even, odd):
    step = pl.program_id(0)
    waves = wave_ref.shape[1]

    def fill(start, buffer):
        for j in range(half // sub):
            at = pl.multiple_of(start + j * sub, sub)
            turns = lax.dot_general(
                pieces(coords_ref[:, pl.ds(at, sub)], COORD_PIECES),
                wave_pieces[...],
                (((0,), (0,)), ((), ())),
                preferred_element_type=jnp.float32,
            )
            cosine, sine = circle(turns)
            buffer[j * sub : (j + 1) * sub, :waves] = cosine.astype(jnp.bfloat16)
            buffer[j * sub : (j + 1) * sub, waves:] = sine.astype(jnp.bfloat16)

    @pl.when(step == 0)
    def _():
        wave_pieces[...] = pieces(wave_ref[...] * TURNS, WAVE_PIECES)
        out_ref[...] = jnp.zeros_like(out_ref)
        fill(0, even)

    here = step * (2 * half)
    fill(here + half, odd)
    out_ref[...] += jnp.dot(shapes_ref[:, :half], even[...], preferred_element_type=jnp.float32)
    fill(jnp.where(step == pl.num_programs(0) - 1, 0, here + 2 * half), even)
    out_ref[...] += jnp.dot(shapes_ref[:, half:], odd[...], preferred_element_type=jnp.float32)


def unit_forces(coords, wavevec, mode_shapes):
    modes, nodes = mode_shapes.shape
    waves = wavevec.shape[1]
    half, sub = 2048, 256
    return pl.pallas_call(
        functools.partial(forces_kernel, half, sub),
        grid=(nodes // (2 * half),),
        in_specs=[
            pl.BlockSpec((3, nodes), lambda i: (0, 0)),
            pl.BlockSpec((3, waves), lambda i: (0, 0)),
            pl.BlockSpec((modes, 2 * half), lambda i: (0, i)),
        ],
        out_specs=pl.BlockSpec((modes, 2 * waves), lambda i: (0, 0)),
        out_shape=jax.ShapeDtypeStruct((modes, 2 * waves), jnp.float32),
        scratch_shapes=[
            pltpu.VMEM((8 * len(WAVE_PIECES), waves), jnp.bfloat16),
            pltpu.VMEM((half, 2 * waves), jnp.bfloat16),
            pltpu.VMEM((half, 2 * waves), jnp.bfloat16),
        ],
        compiler_params=pltpu.CompilerParams(vmem_limit_bytes=48 << 20),
        cost_estimate=pl.CostEstimate(
            flops=4 * modes * nodes * waves, bytes_accessed=2 * modes * nodes, transcendentals=0
        ),
    )(coords, wavevec, mode_shapes)


def modal_response(forces, wave_amp, modal_frf):
    waves = forces.shape[1] // 2
    cosine, sine = forces[:, :waves], forces[:, waves:]
    amp_real, amp_imag = wave_amp[0][None, :], wave_amp[1][None, :]
    force_real = amp_real * cosine - amp_imag * sine
    force_imag = amp_real * sine + amp_imag * cosine
    gain_real, gain_imag = modal_frf[0][:, None], modal_frf[1][:, None]
    modal_real = gain_real * force_real - gain_imag * force_imag
    modal_imag = gain_real * force_imag + gain_imag * force_real
    upper = jnp.concatenate([modal_real, modal_imag], axis=1)
    lower = jnp.concatenate([-modal_imag, modal_real], axis=1)
    return jnp.concatenate([upper, lower], axis=0).astype(jnp.bfloat16)


def cross_spectra(owned_rows, others):
    waves = owned_rows.shape[1] // 2
    turned = jnp.concatenate([owned_rows[:, waves:], -owned_rows[:, :waves]], axis=1)
    stacked = jnp.concatenate([owned_rows, turned], axis=0)
    product = lax.dot_general(
        stacked, others, (((1,), (1,)), ((), ())), preferred_element_type=jnp.float32
    )
    return product.reshape(2, owned_rows.shape[0], others.shape[0]) * (1.0 / waves)


def project_field(transfer, operand):
    return lax.dot_general(
        transfer, operand, (((0,), (0,)), ((), ())), preferred_element_type=jnp.float32
    )


def body(coords, wavevec, wave_amp, mode_shapes, modal_frf, radiation):
    forces = lax.psum(unit_forces(coords, wavevec, mode_shapes), "node")
    operand = modal_response(forces, wave_amp, modal_frf)
    transfer = radiation.reshape(2 * radiation.shape[1], radiation.shape[2])
    owned_rows = lax.psum_scatter(
        project_field(transfer, operand), "mode", scatter_dimension=0, tiled=True
    ).astype(jnp.bfloat16)
    spectra_out = cross_spectra(
        owned_rows, lax.all_gather(owned_rows, ("node", "mode"), axis=0, tiled=True)
    )
    return (spectra_out, owned_rows)


def solution(mesh):
    placed = (
        P(None, "node"),
        P(),
        P(),
        P("mode", "node"),
        P(None, "mode"),
        P(None, "mode", "node"),
    )
    return jax.shard_map(
        body,
        mesh=mesh,
        in_specs=placed,
        out_specs=(P(None, ("node", "mode"), None), P(("node", "mode"), None)),
        check_vma=False,
    )
```

```python
import functools

import jax
import jax.numpy as jnp
from jax import lax
from jax.experimental import pallas as pl
from jax.experimental.pallas import tpu as pltpu
from jax.sharding import PartitionSpec as P

SINE = (4.441535719696892, -7.264680836400963, 3.2520496076552887)
COSINE = (1.414204080330576, -6.977642043687199, 5.715238221214665, -1.7283481089755481)
COORD_PIECES = (0, 0, 1, 1, 0, 2)
WAVE_PIECES = (0, 1, 0, 1, 2, 0)
TURNS = 0.15915494309189535
CHUNKS = 1
BIG = pltpu.CompilerParams(vmem_limit_bytes=48 << 20)


def circle(turns):
    r = turns - jnp.round(turns)
    u = r * r
    s = r * (SINE[0] + u * (SINE[1] + u * SINE[2]))
    c = COSINE[0] + u * (COSINE[1] + u * (COSINE[2] + u * COSINE[3]))
    return c * c - 1.0, s * c


def pieces(x, order):
    first = x.astype(jnp.bfloat16).astype(jnp.float32)
    second = (x - first).astype(jnp.bfloat16).astype(jnp.float32)
    third = x - first - second
    blank = jnp.zeros((8 - x.shape[0], x.shape[1]), jnp.float32)
    parts = [jnp.concatenate([p, blank], axis=0) for p in (first, second, third)]
    return jnp.concatenate([parts[i] for i in order], axis=0).astype(jnp.bfloat16)


def forces_kernel(
    half, sub, coords_ref, wave_ref, shapes_ref, mine_ref, other_ref, wave_pieces, even, odd
):
    step = pl.program_id(0)
    waves = wave_ref.shape[1]
    own = waves // 2

    def fill(start, buffer):
        for j in range(half // sub):
            at = pl.multiple_of(start + j * sub, sub)
            turns = lax.dot_general(
                pieces(coords_ref[:, pl.ds(at, sub)], COORD_PIECES),
                wave_pieces[...],
                (((0,), (0,)), ((), ())),
                preferred_element_type=jnp.float32,
            )
            cosine, sine = (x.astype(jnp.bfloat16) for x in circle(turns))
            rows = slice(j * sub, (j + 1) * sub)
            buffer[rows, :own] = cosine[:, :own]
            buffer[rows, own : 2 * own] = sine[:, :own]
            buffer[rows, 2 * own : 3 * own] = cosine[:, own:]
            buffer[rows, 3 * own :] = sine[:, own:]

    def add(columns, buffer):
        product = jnp.dot(
            shapes_ref[:, columns], buffer[...], preferred_element_type=jnp.float32
        )
        mine_ref[...] += product[:, :waves]
        other_ref[...] += product[:, waves:]

    @pl.when(step == 0)
    def _():
        wave_pieces[...] = pieces(wave_ref[...] * TURNS, WAVE_PIECES)
        mine_ref[...] = jnp.zeros_like(mine_ref)
        other_ref[...] = jnp.zeros_like(other_ref)
        fill(0, even)

    here = step * (2 * half)
    fill(here + half, odd)
    add(slice(0, half), even)
    fill(jnp.where(step == pl.num_programs(0) - 1, 0, here + 2 * half), even)
    add(slice(half, 2 * half), odd)


def unit_forces(coords, wavevec, mode_shapes):
    modes, nodes = mode_shapes.shape
    waves = wavevec.shape[1]
    half, sub = 2048, 256
    out = jax.ShapeDtypeStruct((modes, waves), jnp.float32)
    return pl.pallas_call(
        functools.partial(forces_kernel, half, sub),
        grid=(nodes // (2 * half),),
        in_specs=[
            pl.BlockSpec((3, nodes), lambda i: (0, 0)),
            pl.BlockSpec((3, waves), lambda i: (0, 0)),
            pl.BlockSpec((modes, 2 * half), lambda i: (0, i)),
        ],
        out_specs=[pl.BlockSpec((modes, waves), lambda i: (0, 0))] * 2,
        out_shape=[out, out],
        scratch_shapes=[
            pltpu.VMEM((8 * len(WAVE_PIECES), waves), jnp.bfloat16),
            pltpu.VMEM((half, 2 * waves), jnp.bfloat16),
            pltpu.VMEM((half, 2 * waves), jnp.bfloat16),
        ],
        compiler_params=BIG,
        cost_estimate=pl.CostEstimate(
            flops=12 * modes * nodes * waves, bytes_accessed=2 * modes * nodes, transcendentals=0
        ),
    )(coords, wavevec, mode_shapes)


def field_kernel(
    blocks, kept_ref, last_ref, amp_ref, frf_ref, own_ref, mate_ref, total_ref, *sent_refs
):
    forces = kept_ref[...] + last_ref[...].astype(jnp.float32)
    waves = forces.shape[1] // 2
    cosine, sine = forces[:, :waves], forces[:, waves:]
    amp_real, amp_imag = amp_ref[0:1, :], amp_ref[1:2, :]
    force_real = amp_real * cosine - amp_imag * sine
    force_imag = amp_real * sine + amp_imag * cosine
    gain_real, gain_imag = frf_ref[:, 0:1], frf_ref[:, 1:2]
    real = gain_real * force_real - gain_imag * force_imag
    imag = gain_real * force_imag + gain_imag * force_real
    upper = jnp.concatenate([real, imag], axis=1).astype(jnp.bfloat16)
    lower = jnp.concatenate([-imag, real], axis=1).astype(jnp.bfloat16)
    over_modes = (((0,), (0,)), ((), ()))
    width = own_ref.shape[2] // blocks
    for side, transfer in enumerate((own_ref, mate_ref)):
        field = lax.dot_general(
            upper, transfer[0], over_modes, preferred_element_type=jnp.float32
        ) + lax.dot_general(lower, transfer[1], over_modes, preferred_element_type=jnp.float32)
        total_ref[side] = field[:, :width]
        for k, sent in enumerate(sent_refs):
            sent[side] = field[:, (k + 1) * width : (k + 2) * width].astype(jnp.bfloat16)


def partial_fields(blocks, kept, last, amp, frf, own, mate):
    waves = kept.shape[1]
    shape = (2, waves, own.shape[2] // blocks)
    return pl.pallas_call(
        functools.partial(field_kernel, blocks),
        out_shape=[jax.ShapeDtypeStruct(shape, jnp.float32)]
        + [jax.ShapeDtypeStruct(shape, jnp.bfloat16)] * (blocks - 1),
        compiler_params=BIG,
        cost_estimate=pl.CostEstimate(
            flops=8 * own.shape[1] * own.shape[2] * waves,
            bytes_accessed=4 * own.size,
            transcendentals=0,
        ),
    )(kept, last, amp, frf, own, mate)


def spectra_kernel(chunks, blocks, place_ref, *refs):
    ours = refs[:chunks]
    theirs = refs[chunks : 2 * chunks]
    left_ours = refs[2 * chunks : 3 * chunks]
    left_theirs = refs[3 * chunks : 4 * chunks]
    out_ref, left = refs[-2:]
    depth, rows = ours[0].shape[-2:]
    waves = depth // 2
    first = (pl.program_id(0) == 0) & (pl.program_id(1) == 0)

    @pl.when(first)
    def _():
        for n, ref in enumerate((*left_ours, *left_theirs)):
            turned = ref[...].astype(jnp.float32).T
            real, imag = turned[:, :waves], turned[:, waves:]
            left[n, :rows] = turned.astype(jnp.bfloat16)
            left[n, rows:] = jnp.concatenate([imag, -real], axis=1).astype(jnp.bfloat16)

    scale = 1.0 / (2 * chunks * waves)
    for z in range(blocks):
        at = lax.rem(place_ref[1] - z + blocks, blocks)
        total = 0.0
        for n, ref in enumerate((*ours, *theirs)):
            total = total + jnp.dot(left[n], ref[at, 0], preferred_element_type=jnp.float32)
        out_ref[0, :, z * rows : (z + 1) * rows] = total[:rows] * scale
        out_ref[1, :, z * rows : (z + 1) * rows] = total[rows:] * scale


def cross_spectra(place, blocks, groups, ours, theirs, left_ours, left_theirs):
    chunks = len(ours)
    depth, rows = left_ours[0].shape
    bits = groups.bit_length() - 1

    def at(core_of_data, group, side, place_ref):
        turn = jnp.bitwise_xor(group, place_ref[0])
        flipped = 0
        for b in range(bits):
            flipped = flipped + ((turn >> b) & 1) * (1 << (bits - 1 - b))
        same = jnp.where(core_of_data == 0, turn, flipped)
        return (same, 0, jnp.bitwise_xor(side, core_of_data), 0, 0)

    def of_ours(g, s, place_ref):
        return at(place_ref[2], g, s, place_ref)

    def of_theirs(g, s, place_ref):
        return at(1 - place_ref[2], g, s, place_ref)

    block = (None, blocks, 1, depth, rows)
    whole = pl.BlockSpec((depth, rows), lambda g, s, place_ref: (0, 0))
    return pl.pallas_call(
        functools.partial(spectra_kernel, chunks, blocks),
        grid_spec=pltpu.PrefetchScalarGridSpec(
            num_scalar_prefetch=1,
            grid=(groups, 2),
            in_specs=[pl.BlockSpec(block, of_ours)] * chunks
            + [pl.BlockSpec(block, of_theirs)] * chunks
            + [whole] * (2 * chunks),
            out_specs=pl.BlockSpec(
                (2, rows, blocks * rows), lambda g, s, place_ref: (0, 0, 2 * g + s)
            ),
            scratch_shapes=[pltpu.VMEM((2 * chunks, 2 * rows, depth), jnp.bfloat16)],
        ),
        out_shape=jax.ShapeDtypeStruct((2, rows, 2 * groups * blocks * rows), jnp.float32),
        compiler_params=BIG,
    )(place, *ours, *theirs, *left_ours, *left_theirs)


def body(nodes, blocks, coords, wavevec, wave_amp, mode_shapes, modal_frf, radiation):
    groups = nodes // 2
    bits = groups.bit_length() - 1
    node, mode = lax.axis_index("node"), lax.axis_index("mode")
    core = lax.rem(node, 2)
    place = jnp.stack([node // 2, mode, core]).astype(jnp.int32)

    def to_mate(x):
        return lax.ppermute(x, "node", [(i, i ^ 1) for i in range(nodes)])

    def across(x, step):
        def flip(i):
            return i ^ (2 << (step if i % 2 == 0 else bits - 1 - step))

        return lax.ppermute(x, "node", [(i, flip(i)) for i in range(nodes)])

    def along(x, k):
        return lax.ppermute(x, "mode", [(i, (i + k) % blocks) for i in range(blocks)])

    width = radiation.shape[2] // blocks
    doubled = jnp.concatenate([radiation, radiation[:, :, : (blocks - 1) * width]], axis=2)
    own = lax.dynamic_slice_in_dim(doubled, mode * width, blocks * width, 2)
    mate = to_mate(own)
    frf = modal_frf.T

    size = wavevec.shape[1] // 2 // CHUNKS
    halves = jnp.roll(jnp.stack(jnp.split(wavevec, 2, axis=1)), core, axis=0)
    amps = jnp.where(core == 0, *jnp.split(wave_amp, 2, axis=1))

    ours, theirs, left_ours, left_theirs = [], [], [], []
    for chunk in range(CHUNKS):
        part = slice(chunk * size, (chunk + 1) * size)
        mine, other = unit_forces(
            coords, jnp.concatenate([halves[0, :, part], halves[1, :, part]], axis=1), mode_shapes
        )
        kept = mine + to_mate(other)
        for step in range(bits - 1):
            kept = kept + across(kept.astype(jnp.bfloat16), step).astype(jnp.float32)
        last = across(kept.astype(jnp.bfloat16), bits - 1)
        total, *sent = partial_fields(blocks, kept, last, amps[:, part], frf, own, mate)
        for k, block in enumerate(sent):
            total = total + along(block, k + 1).astype(jnp.float32)
        field = total.astype(jnp.bfloat16)
        column = jnp.stack([field] + [along(field, k) for k in range(1, blocks)])
        gathered = [column]
        for step in range(bits):
            gathered = gathered + [across(x, step) for x in gathered]
        mates = [to_mate(x) for x in gathered]
        ours.append(jnp.stack(gathered))
        theirs.append(jnp.stack(mates))
        left_ours.append(field[0])
        left_theirs.append(mates[0][0, 1])
    spectra = cross_spectra(place, blocks, groups, ours, theirs, left_ours, left_theirs)
    in_order = [
        jnp.where(core == 0, a, b)
        for first, second in ((left_ours, left_theirs), (left_theirs, left_ours))
        for a, b in zip(first, second)
    ]
    field_pressure = jnp.concatenate(
        [x[:size] for x in in_order] + [x[size:] for x in in_order], axis=0
    ).T
    return (spectra, field_pressure)


def solution(mesh):
    placed = (
        P(None, "node"),
        P(),
        P(),
        P("mode", "node"),
        P(None, "mode"),
        P(None, "mode", "node"),
    )
    return jax.shard_map(
        functools.partial(body, mesh.shape["node"], mesh.shape["mode"]),
        mesh=mesh,
        in_specs=placed,
        out_specs=(P(None, ("node", "mode"), None), P(("node", "mode"), None)),
        check_vma=False,
    )
```

```python
import functools

import jax
import jax.numpy as jnp
from jax import lax
from jax.experimental import pallas as pl
from jax.experimental.pallas import tpu as pltpu
from jax.sharding import PartitionSpec as P

SINE = (4.441535719696892, -7.264680836400963, 3.2520496076552887)
COSINE = (1.414204080330576, -6.977642043687199, 5.715238221214665, -1.7283481089755481)
COORD_PIECES = (0, 0, 1, 1, 0, 2)
WAVE_PIECES = (0, 1, 0, 1, 2, 0)
TURNS = 0.15915494309189535
CHUNKS = 2
BIG = pltpu.CompilerParams(vmem_limit_bytes=48 << 20)


def circle(turns):
    r = turns - jnp.round(turns)
    u = r * r
    s = r * (SINE[0] + u * (SINE[1] + u * SINE[2]))
    c = COSINE[0] + u * (COSINE[1] + u * (COSINE[2] + u * COSINE[3]))
    return c * c - 1.0, s * c


def pieces(x, order):
    first = x.astype(jnp.bfloat16).astype(jnp.float32)
    second = (x - first).astype(jnp.bfloat16).astype(jnp.float32)
    third = x - first - second
    blank = jnp.zeros((8 - x.shape[0], x.shape[1]), jnp.float32)
    parts = [jnp.concatenate([p, blank], axis=0) for p in (first, second, third)]
    return jnp.concatenate([parts[i] for i in order], axis=0).astype(jnp.bfloat16)


def forces_kernel(
    piece,
    sub,
    coords_ref,
    wave_ref,
    shapes_ref,
    mine_ref,
    other_ref,
    wave_pieces,
    even_turns,
    odd_turns,
    even,
    odd,
):
    step, steps = pl.program_id(0), pl.num_programs(0)
    waves = wave_ref.shape[1]
    own = waves // 2
    count = shapes_ref.shape[1] // piece
    nodes = coords_ref.shape[1]
    turns, load = (even_turns, odd_turns), (even, odd)

    def phase(start, into):
        for j in range(0, piece, sub):
            at = pl.multiple_of(start + j, sub)
            into[j : j + sub, :] = lax.dot_general(
                pieces(coords_ref[:, pl.ds(at, sub)], COORD_PIECES),
                wave_pieces[...],
                (((0,), (0,)), ((), ())),
                preferred_element_type=jnp.float32,
            )

    def points(angles, into):
        for j in range(0, piece, 64):
            rows = slice(j, j + 64)
            cosine, sine = (x.astype(jnp.bfloat16) for x in circle(angles[rows, :]))
            into[rows, :own] = cosine[:, :own]
            into[rows, own : 2 * own] = sine[:, :own]
            into[rows, 2 * own : 3 * own] = cosine[:, own:]
            into[rows, 3 * own :] = sine[:, own:]

    @pl.when(step == 0)
    def _():
        first, second = wave_ref[:, :own], wave_ref[:, own:]
        swap = lax.rem(lax.axis_index("node"), 2) == 1
        ordered = jnp.concatenate(
            [jnp.where(swap, second, first), jnp.where(swap, first, second)], axis=1
        )
        wave_pieces[...] = pieces(ordered * TURNS, WAVE_PIECES)
        mine_ref[...] = jnp.zeros_like(mine_ref)
        other_ref[...] = jnp.zeros_like(other_ref)
        phase(0, turns[0])
        phase(piece, turns[1])
        points(turns[0], load[0])

    for p in range(count):
        ahead = (step * count + p + 2) * piece
        phase(jnp.where(ahead >= nodes, 0, ahead), turns[p % 2])
        points(turns[(p + 1) % 2], load[(p + 1) % 2])
        product = jnp.dot(
            shapes_ref[:, p * piece : (p + 1) * piece],
            load[p % 2][...],
            preferred_element_type=jnp.float32,
        )
        mine_ref[...] += product[:, :waves]
        other_ref[...] += product[:, waves:]


def unit_forces(coords, wavevec, mode_shapes):
    modes, nodes = mode_shapes.shape
    waves = wavevec.shape[1]
    block, piece, sub = 4096, 1024, 256
    out = jax.ShapeDtypeStruct((modes, waves), jnp.float32)
    return pl.pallas_call(
        functools.partial(forces_kernel, piece, sub),
        grid=(nodes // block,),
        in_specs=[
            pl.BlockSpec((3, nodes), lambda i: (0, 0)),
            pl.BlockSpec((3, waves), lambda i: (0, 0)),
            pl.BlockSpec((modes, block), lambda i: (0, i)),
        ],
        out_specs=[pl.BlockSpec((modes, waves), lambda i: (0, 0))] * 2,
        out_shape=[out, out],
        scratch_shapes=[
            pltpu.VMEM((8 * len(WAVE_PIECES), waves), jnp.bfloat16),
            pltpu.VMEM((piece, waves), jnp.float32),
            pltpu.VMEM((piece, waves), jnp.float32),
            pltpu.VMEM((piece, 2 * waves), jnp.bfloat16),
            pltpu.VMEM((piece, 2 * waves), jnp.bfloat16),
        ],
        compiler_params=BIG,
        cost_estimate=pl.CostEstimate(
            flops=12 * modes * nodes * waves, bytes_accessed=2 * modes * nodes, transcendentals=0
        ),
    )(coords, wavevec, mode_shapes)


def field_kernel(
    blocks, kept_ref, last_ref, amp_ref, frf_ref, own_ref, mate_ref, *refs
):
    totals, sends, whole = refs[:CHUNKS], refs[CHUNKS:-1], refs[-1]
    forces = kept_ref[...] + last_ref[...].astype(jnp.float32)
    waves = forces.shape[1] // 2
    cosine, sine = forces[:, :waves], forces[:, waves:]
    swap = lax.rem(lax.axis_index("node"), 2) == 1
    amp = jnp.where(swap, amp_ref[:, waves:], amp_ref[:, :waves])
    amp_real, amp_imag = amp[0:1, :], amp[1:2, :]
    force_real = amp_real * cosine - amp_imag * sine
    force_imag = amp_real * sine + amp_imag * cosine
    frf = frf_ref[...].T
    gain_real, gain_imag = frf[:, 0:1], frf[:, 1:2]
    real = gain_real * force_real - gain_imag * force_imag
    imag = gain_real * force_imag + gain_imag * force_real
    upper = jnp.concatenate([real, imag], axis=1).astype(jnp.bfloat16)
    lower = jnp.concatenate([-imag, real], axis=1).astype(jnp.bfloat16)
    over_modes = (((0,), (0,)), ((), ()))
    width = own_ref.shape[2] // blocks
    size = waves // CHUNKS
    turned = width % 128 != 0
    for side, transfer in enumerate((own_ref, mate_ref)):
        whole[...] = lax.dot_general(
            upper, transfer[0], over_modes, preferred_element_type=jnp.float32
        ) + lax.dot_general(lower, transfer[1], over_modes, preferred_element_type=jnp.float32)
        for k in range(blocks):
            if turned:
                field = whole[:, k * width : (k + 1) * width]
            else:
                to = lax.rem(lax.axis_index("mode") + k, blocks)
                field = whole[:, pl.ds(pl.multiple_of(to * width, width), width)]
            for c in range(CHUNKS):
                part = jnp.concatenate(
                    [
                        field[c * size : (c + 1) * size],
                        field[waves + c * size : waves + (c + 1) * size],
                    ],
                    axis=0,
                )
                if k == 0:
                    totals[c][side] = part
                else:
                    sends[c * (blocks - 1) + k - 1][side] = part.astype(jnp.bfloat16)


def partial_fields(blocks, kept, last, amp, frf, own, mate):
    waves = kept.shape[1]
    width = own.shape[2] // blocks
    shape = (2, waves // CHUNKS, width)
    if width % 128 != 0:
        mode = lax.axis_index("mode")

        def turn(x):
            doubled = jnp.concatenate([x, x[:, :, : (blocks - 1) * width]], axis=2)
            return lax.dynamic_slice_in_dim(doubled, mode * width, blocks * width, 2)

        own, mate = turn(own), turn(mate)
    out = pl.pallas_call(
        functools.partial(field_kernel, blocks),
        out_shape=[jax.ShapeDtypeStruct(shape, jnp.float32)] * CHUNKS
        + [jax.ShapeDtypeStruct(shape, jnp.bfloat16)] * (CHUNKS * (blocks - 1)),
        scratch_shapes=[pltpu.VMEM((waves, own.shape[2]), jnp.float32)],
        compiler_params=BIG,
        cost_estimate=pl.CostEstimate(
            flops=8 * own.shape[1] * own.shape[2] * waves,
            bytes_accessed=4 * own.size,
            transcendentals=0,
        ),
    )(kept, last, amp, frf, own, mate)
    return out[:CHUNKS], [
        out[CHUNKS + c * (blocks - 1) : CHUNKS + (c + 1) * (blocks - 1)] for c in range(CHUNKS)
    ]


def own_rows_kernel(*refs):
    fields, left, pressure = refs[:-2], refs[-2], refs[-1]
    rows = left.shape[1] // 2
    size = left.shape[2] // 2
    waves = pressure.shape[1] // 2
    swap = lax.rem(lax.axis_index("node"), 2) == 1
    turned = [ref[...].astype(jnp.float32).T for ref in fields]
    for n, field in enumerate(turned):
        real, imag = field[:, :size], field[:, size:]
        left[n, :rows] = field.astype(jnp.bfloat16)
        left[n, rows:] = jnp.concatenate([imag, -real], axis=1).astype(jnp.bfloat16)
    real = [field[:, :size] for field in turned]
    imag = [field[:, size:] for field in turned]
    for part, at in ((real, 0), (imag, waves)):
        ours = jnp.concatenate(part[:CHUNKS], axis=1)
        theirs = jnp.concatenate(part[CHUNKS:], axis=1)
        half = slice(at, at + waves // 2), slice(at + waves // 2, at + waves)
        pressure[:, half[0]] = jnp.where(swap, theirs, ours).astype(jnp.bfloat16)
        pressure[:, half[1]] = jnp.where(swap, ours, theirs).astype(jnp.bfloat16)


def own_rows(fields):
    depth, rows = fields[0].shape
    return pl.pallas_call(
        own_rows_kernel,
        out_shape=[
            jax.ShapeDtypeStruct((len(fields), 2 * rows, depth), jnp.bfloat16),
            jax.ShapeDtypeStruct((rows, len(fields) * depth), jnp.bfloat16),
        ],
        compiler_params=BIG,
    )(*fields)


def spectra_kernel(blocks, place_ref, left_ref, *refs):
    data, out_ref = refs[: 2 * CHUNKS], refs[-1]
    depth, rows = data[0].shape[-2:]
    scale = 1.0 / (CHUNKS * depth)
    for z in range(blocks):
        at = lax.rem(lax.axis_index("mode") - z + blocks, blocks)
        total = 0.0
        for n, ref in enumerate(data):
            total = total + jnp.dot(left_ref[n], ref[at], preferred_element_type=jnp.float32)
        out_ref[0, :, z * rows : (z + 1) * rows] = total[:rows] * scale
        out_ref[1, :, z * rows : (z + 1) * rows] = total[rows:] * scale


def cross_spectra(place, blocks, groups, spectra, left, ours, theirs):
    depth, rows = ours[0].shape[-2:]

    def of_ours(s, place_ref):
        return (0, jnp.bitwise_xor(s, place_ref[1]), 0, 0)

    def of_theirs(s, place_ref):
        return (0, jnp.bitwise_xor(s, 1 - place_ref[1]), 0, 0)

    block = (blocks, None, depth, rows)
    started = spectra is not None
    return pl.pallas_call(
        functools.partial(spectra_kernel, blocks),
        grid_spec=pltpu.PrefetchScalarGridSpec(
            num_scalar_prefetch=1,
            grid=(2,),
            in_specs=[pl.BlockSpec(left.shape, lambda s, place_ref: (0, 0, 0))]
            + [pl.BlockSpec(block, of_ours)] * CHUNKS
            + [pl.BlockSpec(block, of_theirs)] * CHUNKS
            + [pl.BlockSpec(memory_space=pl.ANY)] * started,
            out_specs=pl.BlockSpec(
                (2, rows, blocks * rows), lambda s, place_ref: (0, 0, 2 * place_ref[0] + s)
            ),
        ),
        out_shape=jax.ShapeDtypeStruct((2, rows, 2 * groups * blocks * rows), jnp.float32),
        input_output_aliases={2 + 2 * CHUNKS: 0} if started else {},
        compiler_params=BIG,
        cost_estimate=pl.CostEstimate(
            flops=8 * CHUNKS * depth * rows * rows * blocks,
            bytes_accessed=32 * rows * rows * blocks,
            transcendentals=0,
        ),
    )(place, left, *ours, *theirs, *([spectra] if started else []))


def body(nodes, blocks, coords, wavevec, wave_amp, mode_shapes, modal_frf, radiation):
    groups = nodes // 2
    bits = groups.bit_length() - 1
    node = lax.axis_index("node")
    group, core = node // 2, lax.rem(node, 2)

    def reverse(p):
        return sum(((p >> b) & 1) << (bits - 1 - b) for b in range(bits))

    def to_mate(x):
        return lax.ppermute(x, "node", [(i, i ^ 1) for i in range(nodes)])

    def across(x, step):
        def flip(i):
            return i ^ (2 << (step if i % 2 == 0 else bits - 1 - step))

        return lax.ppermute(x, "node", [(i, flip(i)) for i in range(nodes)])

    def along(x, k):
        return lax.ppermute(x, "mode", [(i, (i + k) % blocks) for i in range(blocks)])

    mate = to_mate(radiation)
    mine, other = unit_forces(coords, wavevec, mode_shapes)
    kept = mine + to_mate(other)
    for step in range(bits - 1):
        kept = kept + across(kept.astype(jnp.bfloat16), step).astype(jnp.float32)
    last = across(kept.astype(jnp.bfloat16), bits - 1)
    totals, sends = partial_fields(blocks, kept, last, wave_amp, modal_frf, radiation, mate)

    fields, gathered, mates = [], [], []
    for total, sent in zip(totals, sends):
        for k, block in enumerate(sent):
            total = total + along(block, k + 1).astype(jnp.float32)
        fields.append(total.astype(jnp.bfloat16))
    for field in fields:
        parts = [jnp.stack([field] + [along(field, k) for k in range(1, blocks)])]
        for step in range(bits):
            parts = parts + [across(x, step) for x in parts]
        gathered.append(parts)
        mates.append([to_mate(x) for x in parts])
    left, field_pressure = own_rows(
        [field[0] for field in fields] + [parts[0][0, 1] for parts in mates]
    )
    spectra = None
    for p in range(groups):
        at = jnp.bitwise_xor(group, jnp.where(core == 0, p, reverse(p)))
        spectra = cross_spectra(
            jnp.stack([at, core]).astype(jnp.int32),
            blocks,
            groups,
            spectra,
            left,
            [parts[p] for parts in gathered],
            [parts[reverse(p)] for parts in mates],
        )
    return (spectra, field_pressure)


def solution(mesh):
    placed = (
        P(None, "node"),
        P(),
        P(),
        P("mode", "node"),
        P(None, "mode"),
        P(None, "mode", "node"),
    )
    return jax.shard_map(
        functools.partial(body, mesh.shape["node"], mesh.shape["mode"]),
        mesh=mesh,
        in_specs=placed,
        out_specs=(P(None, ("node", "mode"), None), P(("node", "mode"), None)),
        check_vma=False,
    )
```

```python
import functools

import jax
import jax.numpy as jnp
from jax import lax
from jax.experimental import pallas as pl
from jax.experimental.pallas import tpu as pltpu
from jax.sharding import PartitionSpec as P

SINE = (4.441535719696892, -7.264680836400963, 3.2520496076552887)
COSINE = (1.414204080330576, -6.977642043687199, 5.715238221214665, -1.7283481089755481)
COORD_PIECES = (0, 0, 1, 1, 0, 2)
WAVE_PIECES = (0, 1, 0, 1, 2, 0)
TURNS = 0.15915494309189535
CHUNKS = 2
BIG = pltpu.CompilerParams(vmem_limit_bytes=48 << 20)


def circle(turns):
    r = turns - jnp.round(turns)
    u = r * r
    s = r * (SINE[0] + u * (SINE[1] + u * SINE[2]))
    c = COSINE[0] + u * (COSINE[1] + u * (COSINE[2] + u * COSINE[3]))
    return c * c - 1.0, s * c


def pieces(x, order):
    first = x.astype(jnp.bfloat16).astype(jnp.float32)
    second = (x - first).astype(jnp.bfloat16).astype(jnp.float32)
    third = x - first - second
    blank = jnp.zeros((8 - x.shape[0], x.shape[1]), jnp.float32)
    parts = [jnp.concatenate([p, blank], axis=0) for p in (first, second, third)]
    return jnp.concatenate([parts[i] for i in order], axis=0).astype(jnp.bfloat16)


def forces_kernel(
    piece,
    sub,
    coords_ref,
    wave_ref,
    shapes_ref,
    mine_ref,
    other_ref,
    wave_pieces,
    even_turns,
    odd_turns,
    even,
    odd,
):
    step, steps = pl.program_id(0), pl.num_programs(0)
    waves = wave_ref.shape[1]
    own = waves // 2
    count = shapes_ref.shape[1] // piece
    nodes = coords_ref.shape[1]
    turns, load = (even_turns, odd_turns), (even, odd)

    def phase(start, into):
        for j in range(0, piece, sub):
            at = pl.multiple_of(start + j, sub)
            into[j : j + sub, :] = lax.dot_general(
                pieces(coords_ref[:, pl.ds(at, sub)], COORD_PIECES),
                wave_pieces[...],
                (((0,), (0,)), ((), ())),
                preferred_element_type=jnp.float32,
            )

    def points(angles, into):
        for j in range(0, piece, 64):
            rows = slice(j, j + 64)
            cosine, sine = (x.astype(jnp.bfloat16) for x in circle(angles[rows, :]))
            into[rows, :own] = cosine[:, :own]
            into[rows, own : 2 * own] = sine[:, :own]
            into[rows, 2 * own : 3 * own] = cosine[:, own:]
            into[rows, 3 * own :] = sine[:, own:]

    @pl.when(step == 0)
    def _():
        first, second = wave_ref[:, :own], wave_ref[:, own:]
        swap = lax.rem(lax.axis_index("node"), 2) == 1
        ordered = jnp.concatenate(
            [jnp.where(swap, second, first), jnp.where(swap, first, second)], axis=1
        )
        wave_pieces[...] = pieces(ordered * TURNS, WAVE_PIECES)
        mine_ref[...] = jnp.zeros_like(mine_ref)
        other_ref[...] = jnp.zeros_like(other_ref)
        phase(0, turns[0])
        phase(piece, turns[1])
        points(turns[0], load[0])

    for p in range(count):
        ahead = (step * count + p + 2) * piece
        phase(jnp.where(ahead >= nodes, 0, ahead), turns[p % 2])
        points(turns[(p + 1) % 2], load[(p + 1) % 2])
        product = jnp.dot(
            shapes_ref[:, p * piece : (p + 1) * piece],
            load[p % 2][...],
            preferred_element_type=jnp.float32,
        )
        mine_ref[...] += product[:, :waves]
        other_ref[...] += product[:, waves:]


def unit_forces(coords, wavevec, mode_shapes):
    modes, nodes = mode_shapes.shape
    waves = wavevec.shape[1]
    block, piece, sub = 4096, 1024, 1024
    out = jax.ShapeDtypeStruct((modes, waves), jnp.float32)
    return pl.pallas_call(
        functools.partial(forces_kernel, piece, sub),
        grid=(nodes // block,),
        in_specs=[
            pl.BlockSpec((3, nodes), lambda i: (0, 0)),
            pl.BlockSpec((3, waves), lambda i: (0, 0)),
            pl.BlockSpec((modes, block), lambda i: (0, i)),
        ],
        out_specs=[pl.BlockSpec((modes, waves), lambda i: (0, 0))] * 2,
        out_shape=[out, out],
        scratch_shapes=[
            pltpu.VMEM((8 * len(WAVE_PIECES), waves), jnp.bfloat16),
            pltpu.VMEM((piece, waves), jnp.float32),
            pltpu.VMEM((piece, waves), jnp.float32),
            pltpu.VMEM((piece, 2 * waves), jnp.bfloat16),
            pltpu.VMEM((piece, 2 * waves), jnp.bfloat16),
        ],
        compiler_params=pltpu.CompilerParams(vmem_limit_bytes=60 << 20),
        cost_estimate=pl.CostEstimate(
            flops=12 * modes * nodes * waves, bytes_accessed=2 * modes * nodes, transcendentals=0
        ),
    )(coords, wavevec, mode_shapes)


def field_kernel(
    blocks, kept_ref, last_ref, amp_ref, frf_ref, own_ref, mate_ref, *refs
):
    totals, sends, whole = refs[:CHUNKS], refs[CHUNKS:-1], refs[-1]
    forces = kept_ref[...] + last_ref[...].astype(jnp.float32)
    waves = forces.shape[1] // 2
    cosine, sine = forces[:, :waves], forces[:, waves:]
    swap = lax.rem(lax.axis_index("node"), 2) == 1
    amp = jnp.where(swap, amp_ref[:, waves:], amp_ref[:, :waves])
    amp_real, amp_imag = amp[0:1, :], amp[1:2, :]
    force_real = amp_real * cosine - amp_imag * sine
    force_imag = amp_real * sine + amp_imag * cosine
    frf = frf_ref[...].T
    gain_real, gain_imag = frf[:, 0:1], frf[:, 1:2]
    real = gain_real * force_real - gain_imag * force_imag
    imag = gain_real * force_imag + gain_imag * force_real
    upper = jnp.concatenate([real, imag], axis=1).astype(jnp.bfloat16)
    lower = jnp.concatenate([-imag, real], axis=1).astype(jnp.bfloat16)
    over_modes = (((0,), (0,)), ((), ()))
    width = own_ref.shape[2] // blocks
    size = waves // CHUNKS
    turned = width % 128 != 0
    for side, transfer in enumerate((own_ref, mate_ref)):
        whole[...] = lax.dot_general(
            upper, transfer[0], over_modes, preferred_element_type=jnp.float32
        ) + lax.dot_general(lower, transfer[1], over_modes, preferred_element_type=jnp.float32)
        for k in range(blocks):
            if turned:
                field = whole[:, k * width : (k + 1) * width]
            else:
                to = lax.rem(lax.axis_index("mode") + k, blocks)
                field = whole[:, pl.ds(pl.multiple_of(to * width, width), width)]
            for c in range(CHUNKS):
                part = jnp.concatenate(
                    [
                        field[c * size : (c + 1) * size],
                        field[waves + c * size : waves + (c + 1) * size],
                    ],
                    axis=0,
                )
                if k == 0:
                    totals[c][side] = part
                else:
                    sends[c * (blocks - 1) + k - 1][side] = part.astype(jnp.bfloat16)


def partial_fields(blocks, kept, last, amp, frf, own, mate):
    waves = kept.shape[1]
    width = own.shape[2] // blocks
    shape = (2, waves // CHUNKS, width)
    if width % 128 != 0:
        mode = lax.axis_index("mode")

        def turn(x):
            doubled = jnp.concatenate([x, x[:, :, : (blocks - 1) * width]], axis=2)
            return lax.dynamic_slice_in_dim(doubled, mode * width, blocks * width, 2)

        own, mate = turn(own), turn(mate)
    out = pl.pallas_call(
        functools.partial(field_kernel, blocks),
        out_shape=[jax.ShapeDtypeStruct(shape, jnp.float32)] * CHUNKS
        + [jax.ShapeDtypeStruct(shape, jnp.bfloat16)] * (CHUNKS * (blocks - 1)),
        scratch_shapes=[pltpu.VMEM((waves, own.shape[2]), jnp.float32)],
        compiler_params=BIG,
        cost_estimate=pl.CostEstimate(
            flops=8 * own.shape[1] * own.shape[2] * waves,
            bytes_accessed=4 * own.size,
            transcendentals=0,
        ),
    )(kept, last, amp, frf, own, mate)
    return out[:CHUNKS], [
        out[CHUNKS + c * (blocks - 1) : CHUNKS + (c + 1) * (blocks - 1)] for c in range(CHUNKS)
    ]


def own_rows_kernel(*refs):
    fields, left, pressure = refs[:-2], refs[-2], refs[-1]
    rows = left.shape[1] // 2
    size = left.shape[2] // 2
    waves = pressure.shape[1] // 2
    swap = lax.rem(lax.axis_index("node"), 2) == 1
    turned = [ref[...].astype(jnp.float32).T for ref in fields]
    for n, field in enumerate(turned):
        real, imag = field[:, :size], field[:, size:]
        left[n, :rows] = field.astype(jnp.bfloat16)
        left[n, rows:] = jnp.concatenate([imag, -real], axis=1).astype(jnp.bfloat16)
    real = [field[:, :size] for field in turned]
    imag = [field[:, size:] for field in turned]
    for part, at in ((real, 0), (imag, waves)):
        ours = jnp.concatenate(part[:CHUNKS], axis=1)
        theirs = jnp.concatenate(part[CHUNKS:], axis=1)
        half = slice(at, at + waves // 2), slice(at + waves // 2, at + waves)
        pressure[:, half[0]] = jnp.where(swap, theirs, ours).astype(jnp.bfloat16)
        pressure[:, half[1]] = jnp.where(swap, ours, theirs).astype(jnp.bfloat16)


def own_rows(fields):
    depth, rows = fields[0].shape
    return pl.pallas_call(
        own_rows_kernel,
        out_shape=[
            jax.ShapeDtypeStruct((len(fields), 2 * rows, depth), jnp.bfloat16),
            jax.ShapeDtypeStruct((rows, len(fields) * depth), jnp.bfloat16),
        ],
        compiler_params=BIG,
    )(*fields)


def spectra_kernel(blocks, place_ref, left_ref, *refs):
    data, out_ref = refs[: 2 * CHUNKS], refs[-1]
    depth, rows = data[0].shape[-2:]
    mode = lax.axis_index("mode")
    order = [lax.rem(mode - z + blocks, blocks) for z in range(blocks)]
    right = jnp.concatenate(
        [jnp.concatenate([ref[at] for at in order], axis=1) for ref in data], axis=0
    )
    left = jnp.concatenate([left_ref[n] for n in range(len(data))], axis=1)
    total = jnp.dot(left, right, preferred_element_type=jnp.float32) * (1.0 / (CHUNKS * depth))
    out_ref[0] = total[:rows]
    out_ref[1] = total[rows:]


def cross_spectra(place, blocks, groups, spectra, left, ours, theirs):
    depth, rows = ours[0].shape[-2:]

    def of_ours(s, place_ref):
        return (0, jnp.bitwise_xor(s, place_ref[1]), 0, 0)

    def of_theirs(s, place_ref):
        return (0, jnp.bitwise_xor(s, 1 - place_ref[1]), 0, 0)

    block = (blocks, None, depth, rows)
    started = spectra is not None
    return pl.pallas_call(
        functools.partial(spectra_kernel, blocks),
        grid_spec=pltpu.PrefetchScalarGridSpec(
            num_scalar_prefetch=1,
            grid=(2,),
            in_specs=[pl.BlockSpec(left.shape, lambda s, place_ref: (0, 0, 0))]
            + [pl.BlockSpec(block, of_ours)] * CHUNKS
            + [pl.BlockSpec(block, of_theirs)] * CHUNKS
            + [pl.BlockSpec(memory_space=pl.ANY)] * started,
            out_specs=pl.BlockSpec(
                (2, rows, blocks * rows), lambda s, place_ref: (0, 0, 2 * place_ref[0] + s)
            ),
        ),
        out_shape=jax.ShapeDtypeStruct((2, rows, 2 * groups * blocks * rows), jnp.float32),
        input_output_aliases={2 + 2 * CHUNKS: 0} if started else {},
        compiler_params=BIG,
        cost_estimate=pl.CostEstimate(
            flops=160 * CHUNKS * depth * rows * rows * blocks,
            bytes_accessed=32 * rows * rows * blocks,
            transcendentals=0,
        ),
    )(place, left, *ours, *theirs, *([spectra] if started else []))


def body(nodes, blocks, coords, wavevec, wave_amp, mode_shapes, modal_frf, radiation):
    groups = nodes // 2
    bits = groups.bit_length() - 1
    node = lax.axis_index("node")
    group, core = node // 2, lax.rem(node, 2)

    def reverse(p):
        return sum(((p >> b) & 1) << (bits - 1 - b) for b in range(bits))

    def to_mate(x):
        return lax.ppermute(x, "node", [(i, i ^ 1) for i in range(nodes)])

    def across(x, step):
        def flip(i):
            return i ^ (2 << (step if i % 2 == 0 else bits - 1 - step))

        return lax.ppermute(x, "node", [(i, flip(i)) for i in range(nodes)])

    def along(x, k):
        return lax.ppermute(x, "mode", [(i, (i + k) % blocks) for i in range(blocks)])

    mate = to_mate(radiation)
    mine, other = unit_forces(coords, wavevec, mode_shapes)
    kept = mine + to_mate(other)
    for step in range(bits - 1):
        kept = kept + across(kept.astype(jnp.bfloat16), step).astype(jnp.float32)
    last = across(kept.astype(jnp.bfloat16), bits - 1)
    totals, sends = partial_fields(blocks, kept, last, wave_amp, modal_frf, radiation, mate)

    fields = []
    for total, sent in zip(totals, sends):
        for k, block in enumerate(sent):
            total = total + along(block, k + 1).astype(jnp.float32)
        fields.append(total.astype(jnp.bfloat16))
    gathered = [
        [jnp.stack([field] + [along(field, k) for k in range(1, blocks)])] for field in fields
    ]
    mates = [[to_mate(x) for x in parts] for parts in gathered]
    left, field_pressure = own_rows([x[0] for x in fields] + [x[0][0, 1] for x in mates])

    def add_part(spectra, p):
        at = jnp.bitwise_xor(group, jnp.where(core == 0, p, reverse(p)))
        return cross_spectra(
            jnp.stack([at, core]).astype(jnp.int32),
            blocks,
            groups,
            spectra,
            left,
            [parts[p] for parts in gathered],
            [parts[reverse(p)] for parts in mates],
        )

    spectra = add_part(None, 0)
    for step in range(bits):
        for parts in gathered:
            parts += [across(x, step) for x in parts]
    for parts, arrived in zip(mates, gathered):
        parts += [to_mate(x) for x in arrived[1:-1]]
    for p in range(1, groups - 1):
        spectra = add_part(spectra, p)
    spectra, lasts = lax.optimization_barrier((spectra, [parts[-1] for parts in gathered]))
    for c in range(CHUNKS):
        gathered[c][-1] = lasts[c]
        mates[c].append(to_mate(lasts[c]))
    spectra = add_part(spectra, groups - 1)
    return (spectra, field_pressure)


def solution(mesh):
    placed = (
        P(None, "node"),
        P(),
        P(),
        P("mode", "node"),
        P(None, "mode"),
        P(None, "mode", "node"),
    )
    return jax.shard_map(
        functools.partial(body, mesh.shape["node"], mesh.shape["mode"]),
        mesh=mesh,
        in_specs=placed,
        out_specs=(P(None, ("node", "mode"), None), P(("node", "mode"), None)),
        check_vma=False,
    )
```

```python
import functools

import jax
import jax.numpy as jnp
from jax import lax
from jax.experimental import pallas as pl
from jax.experimental.pallas import tpu as pltpu
from jax.sharding import PartitionSpec as P

SINE = (4.441535719696892, -7.264680836400963, 3.2520496076552887)
COSINE = (1.414204080330576, -6.977642043687199, 5.715238221214665, -1.7283481089755481)
COORD_PIECES = (0, 0, 1, 1, 0, 2)
WAVE_PIECES = (0, 1, 0, 1, 2, 0)
TURNS = 0.15915494309189535
CHUNKS = 2
ROWS, LANES, DIRECT = 32, 256, 1
BIG = pltpu.CompilerParams(vmem_limit_bytes=48 << 20)


def circle(turns):
    r = turns - jnp.round(turns)
    u = r * r
    s = r * (SINE[0] + u * (SINE[1] + u * SINE[2]))
    c = COSINE[0] + u * (COSINE[1] + u * (COSINE[2] + u * COSINE[3]))
    return c * c - 1.0, s * c


def pieces(x, order):
    first = x.astype(jnp.bfloat16).astype(jnp.float32)
    second = (x - first).astype(jnp.bfloat16).astype(jnp.float32)
    third = x - first - second
    blank = jnp.zeros((8 - x.shape[0], x.shape[1]), jnp.float32)
    parts = [jnp.concatenate([p, blank], axis=0) for p in (first, second, third)]
    return jnp.concatenate([parts[i] for i in order], axis=0).astype(jnp.bfloat16)


def forces_kernel(
    piece,
    coords_ref,
    wave_ref,
    shapes_ref,
    mine_ref,
    other_ref,
    spread,
    wave_pieces,
    even_turns,
    odd_turns,
    even,
    odd,
):
    step = pl.program_id(0)
    waves = wave_ref.shape[1]
    own = waves // 2
    count = shapes_ref.shape[1] // piece
    nodes = coords_ref.shape[1]
    turns, load = (even_turns, odd_turns), (even, odd)
    direct = DIRECT * LANES

    def phase(start, into):
        at = pl.multiple_of(start + direct, LANES)
        into[...] = jnp.dot(
            wave_pieces[...],
            pieces(coords_ref[:, pl.ds(at, piece - direct)], COORD_PIECES),
            preferred_element_type=jnp.float32,
        )

    def points(start, angles, into):
        for j in range(0, piece, LANES):
            columns = slice(j, j + LANES)
            if j < direct:
                at = pl.multiple_of(start + j, LANES)
                x, y, z = (coords_ref[i : i + 1, pl.ds(at, LANES)] for i in range(3))
            for w in range(0, waves, ROWS):
                rows = slice(w, w + ROWS)
                if j < direct:
                    a, b, c = (spread[i, rows, :] for i in range(3))
                    angle = a * x + b * y + c * z
                else:
                    angle = angles[rows, j - direct : j - direct + LANES]
                cosine, sine = circle(angle)
                to = w if w < own else w + own
                into[to : to + ROWS, columns] = cosine.astype(jnp.bfloat16)
                into[to + own : to + own + ROWS, columns] = sine.astype(jnp.bfloat16)

    @pl.when(step == 0)
    def _():
        first, second = wave_ref[:, :own], wave_ref[:, own:]
        swap = lax.rem(lax.axis_index("node"), 2) == 1
        ordered = TURNS * jnp.concatenate(
            [jnp.where(swap, second, first), jnp.where(swap, first, second)], axis=1
        )
        wave_pieces[...] = pieces(ordered, WAVE_PIECES).astype(jnp.float32).T.astype(jnp.bfloat16)
        columns = jnp.concatenate([ordered, jnp.zeros((5, waves), jnp.float32)], axis=0).T
        for i in range(3):
            spread[i] = jnp.broadcast_to(columns[:, i : i + 1], (waves, LANES))
        mine_ref[...] = jnp.zeros_like(mine_ref)
        other_ref[...] = jnp.zeros_like(other_ref)
        phase(0, turns[0])
        phase(piece, turns[1])
        points(0, turns[0], load[0])

    def wrapped(start):
        return jnp.where(start >= nodes, 0, start)

    for p in range(count):
        here = (step * count + p) * piece
        phase(wrapped(here + 2 * piece), turns[p % 2])
        points(wrapped(here + piece), turns[(p + 1) % 2], load[(p + 1) % 2])
        product = lax.dot_general(
            shapes_ref[:, p * piece : (p + 1) * piece],
            load[p % 2][...],
            (((1,), (1,)), ((), ())),
            preferred_element_type=jnp.float32,
        )
        mine_ref[...] += product[:, :waves]
        other_ref[...] += product[:, waves:]


def unit_forces(coords, wavevec, mode_shapes):
    modes, nodes = mode_shapes.shape
    waves = wavevec.shape[1]
    block, piece = 4096, 1024
    out = jax.ShapeDtypeStruct((modes, waves), jnp.float32)
    return pl.pallas_call(
        functools.partial(forces_kernel, piece),
        grid=(nodes // block,),
        in_specs=[
            pl.BlockSpec((3, nodes), lambda i: (0, 0)),
            pl.BlockSpec((3, waves), lambda i: (0, 0)),
            pl.BlockSpec((modes, block), lambda i: (0, i)),
        ],
        out_specs=[pl.BlockSpec((modes, waves), lambda i: (0, 0))] * 2,
        out_shape=[out, out],
        scratch_shapes=[
            pltpu.VMEM((3, waves, LANES), jnp.float32),
            pltpu.VMEM((waves, 8 * len(WAVE_PIECES)), jnp.bfloat16),
            pltpu.VMEM((waves, piece - DIRECT * LANES), jnp.float32),
            pltpu.VMEM((waves, piece - DIRECT * LANES), jnp.float32),
            pltpu.VMEM((2 * waves, piece), jnp.bfloat16),
            pltpu.VMEM((2 * waves, piece), jnp.bfloat16),
        ],
        compiler_params=pltpu.CompilerParams(vmem_limit_bytes=60 << 20),
        cost_estimate=pl.CostEstimate(
            flops=12 * modes * nodes * waves, bytes_accessed=2 * modes * nodes, transcendentals=0
        ),
    )(coords, wavevec, mode_shapes)


def field_kernel(
    blocks, kept_ref, last_ref, amp_ref, frf_ref, own_ref, mate_ref, *refs
):
    totals, sends, whole = refs[:CHUNKS], refs[CHUNKS:-1], refs[-1]
    forces = kept_ref[...] + last_ref[...].astype(jnp.float32)
    waves = forces.shape[1] // 2
    cosine, sine = forces[:, :waves], forces[:, waves:]
    swap = lax.rem(lax.axis_index("node"), 2) == 1
    amp = jnp.where(swap, amp_ref[:, waves:], amp_ref[:, :waves])
    amp_real, amp_imag = amp[0:1, :], amp[1:2, :]
    force_real = amp_real * cosine - amp_imag * sine
    force_imag = amp_real * sine + amp_imag * cosine
    frf = frf_ref[...].T
    gain_real, gain_imag = frf[:, 0:1], frf[:, 1:2]
    real = gain_real * force_real - gain_imag * force_imag
    imag = gain_real * force_imag + gain_imag * force_real
    upper = jnp.concatenate([real, imag], axis=1).astype(jnp.bfloat16)
    lower = jnp.concatenate([-imag, real], axis=1).astype(jnp.bfloat16)
    over_modes = (((0,), (0,)), ((), ()))
    width = own_ref.shape[2] // blocks
    size = waves // CHUNKS
    turned = width % 128 != 0
    for side, transfer in enumerate((own_ref, mate_ref)):
        whole[...] = lax.dot_general(
            upper, transfer[0], over_modes, preferred_element_type=jnp.float32
        ) + lax.dot_general(lower, transfer[1], over_modes, preferred_element_type=jnp.float32)
        for k in range(blocks):
            if turned:
                field = whole[:, k * width : (k + 1) * width]
            else:
                to = lax.rem(lax.axis_index("mode") + k, blocks)
                field = whole[:, pl.ds(pl.multiple_of(to * width, width), width)]
            for c in range(CHUNKS):
                part = jnp.concatenate(
                    [
                        field[c * size : (c + 1) * size],
                        field[waves + c * size : waves + (c + 1) * size],
                    ],
                    axis=0,
                )
                if k == 0:
                    totals[c][side] = part
                else:
                    sends[c * (blocks - 1) + k - 1][side] = part.astype(jnp.bfloat16)


def partial_fields(blocks, kept, last, amp, frf, own, mate):
    waves = kept.shape[1]
    width = own.shape[2] // blocks
    shape = (2, waves // CHUNKS, width)
    if width % 128 != 0:
        mode = lax.axis_index("mode")

        def turn(x):
            doubled = jnp.concatenate([x, x[:, :, : (blocks - 1) * width]], axis=2)
            return lax.dynamic_slice_in_dim(doubled, mode * width, blocks * width, 2)

        own, mate = turn(own), turn(mate)
    out = pl.pallas_call(
        functools.partial(field_kernel, blocks),
        out_shape=[jax.ShapeDtypeStruct(shape, jnp.float32)] * CHUNKS
        + [jax.ShapeDtypeStruct(shape, jnp.bfloat16)] * (CHUNKS * (blocks - 1)),
        scratch_shapes=[pltpu.VMEM((waves, own.shape[2]), jnp.float32)],
        compiler_params=BIG,
        cost_estimate=pl.CostEstimate(
            flops=8 * own.shape[1] * own.shape[2] * waves,
            bytes_accessed=4 * own.size,
            transcendentals=0,
        ),
    )(kept, last, amp, frf, own, mate)
    return out[:CHUNKS], [
        out[CHUNKS + c * (blocks - 1) : CHUNKS + (c + 1) * (blocks - 1)] for c in range(CHUNKS)
    ]


def own_rows_kernel(*refs):
    fields, left, pressure = refs[:-2], refs[-2], refs[-1]
    rows = left.shape[1] // 2
    size = left.shape[2] // 2
    waves = pressure.shape[1] // 2
    swap = lax.rem(lax.axis_index("node"), 2) == 1
    turned = [ref[...].astype(jnp.float32).T for ref in fields]
    for n, field in enumerate(turned):
        real, imag = field[:, :size], field[:, size:]
        left[n, :rows] = field.astype(jnp.bfloat16)
        left[n, rows:] = jnp.concatenate([imag, -real], axis=1).astype(jnp.bfloat16)
    real = [field[:, :size] for field in turned]
    imag = [field[:, size:] for field in turned]
    for part, at in ((real, 0), (imag, waves)):
        ours = jnp.concatenate(part[:CHUNKS], axis=1)
        theirs = jnp.concatenate(part[CHUNKS:], axis=1)
        half = slice(at, at + waves // 2), slice(at + waves // 2, at + waves)
        pressure[:, half[0]] = jnp.where(swap, theirs, ours).astype(jnp.bfloat16)
        pressure[:, half[1]] = jnp.where(swap, ours, theirs).astype(jnp.bfloat16)


def own_rows(fields):
    depth, rows = fields[0].shape
    return pl.pallas_call(
        own_rows_kernel,
        out_shape=[
            jax.ShapeDtypeStruct((len(fields), 2 * rows, depth), jnp.bfloat16),
            jax.ShapeDtypeStruct((rows, len(fields) * depth), jnp.bfloat16),
        ],
        compiler_params=BIG,
    )(*fields)


def spectra_kernel(blocks, place_ref, left_ref, *refs):
    data, out_ref = refs[: 2 * CHUNKS], refs[-1]
    depth, rows = data[0].shape[-2:]
    mode = lax.axis_index("mode")
    order = [lax.rem(mode - z + blocks, blocks) for z in range(blocks)]
    left = jnp.concatenate([left_ref[n] for n in range(len(data))], axis=1)
    for side in range(2):
        sides = [jnp.bitwise_xor(side, place_ref[1]), jnp.bitwise_xor(side, 1 - place_ref[1])]
        right = jnp.concatenate(
            [
                jnp.concatenate([ref[at, sides[n // CHUNKS]] for at in order], axis=1)
                for n, ref in enumerate(data)
            ],
            axis=0,
        )
        total = jnp.dot(left, right, preferred_element_type=jnp.float32) * (1.0 / (CHUNKS * depth))
        columns = slice(side * blocks * rows, (side + 1) * blocks * rows)
        out_ref[0, :, columns] = total[:rows]
        out_ref[1, :, columns] = total[rows:]


def cross_spectra(place, blocks, groups, spectra, left, ours, theirs):
    depth, rows = ours[0].shape[-2:]
    started = spectra is not None
    return pl.pallas_call(
        functools.partial(spectra_kernel, blocks),
        grid_spec=pltpu.PrefetchScalarGridSpec(
            num_scalar_prefetch=1,
            grid=(1,),
            in_specs=[pl.BlockSpec(left.shape, lambda s, place_ref: (0, 0, 0))]
            + [pl.BlockSpec(ours[0].shape, lambda s, place_ref: (0, 0, 0, 0))] * (2 * CHUNKS)
            + [pl.BlockSpec(memory_space=pl.ANY)] * started,
            out_specs=pl.BlockSpec(
                (2, rows, 2 * blocks * rows), lambda s, place_ref: (0, 0, place_ref[0])
            ),
        ),
        out_shape=jax.ShapeDtypeStruct((2, rows, 2 * groups * blocks * rows), jnp.float32),
        input_output_aliases={2 + 2 * CHUNKS: 0} if started else {},
        compiler_params=BIG,
        cost_estimate=pl.CostEstimate(
            flops=160 * CHUNKS * depth * rows * rows * blocks,
            bytes_accessed=32 * rows * rows * blocks,
            transcendentals=0,
        ),
    )(place, left, *ours, *theirs, *([spectra] if started else []))


def body(nodes, blocks, coords, wavevec, wave_amp, mode_shapes, modal_frf, radiation):
    groups = nodes // 2
    bits = groups.bit_length() - 1
    node = lax.axis_index("node")
    group, core = node // 2, lax.rem(node, 2)

    def reverse(p):
        return sum(((p >> b) & 1) << (bits - 1 - b) for b in range(bits))

    def to_mate(x):
        return lax.ppermute(x, "node", [(i, i ^ 1) for i in range(nodes)])

    def across(x, step):
        def flip(i):
            return i ^ (2 << (step if i % 2 == 0 else bits - 1 - step))

        return lax.ppermute(x, "node", [(i, flip(i)) for i in range(nodes)])

    def along(x, k):
        return lax.ppermute(x, "mode", [(i, (i + k) % blocks) for i in range(blocks)])

    mate = to_mate(radiation)
    mine, other = unit_forces(coords, wavevec, mode_shapes)
    kept = mine + to_mate(other)
    for step in range(bits - 1):
        kept = kept + across(kept.astype(jnp.bfloat16), step).astype(jnp.float32)
    last = across(kept.astype(jnp.bfloat16), bits - 1)
    totals, sends = partial_fields(blocks, kept, last, wave_amp, modal_frf, radiation, mate)

    fields = []
    for total, sent in zip(totals, sends):
        for k, block in enumerate(sent):
            total = total + along(block, k + 1).astype(jnp.float32)
        fields.append(total.astype(jnp.bfloat16))
    gathered = [
        [jnp.stack([field] + [along(field, k) for k in range(1, blocks)])] for field in fields
    ]
    mates = [[to_mate(x) for x in parts] for parts in gathered]
    left, field_pressure = own_rows([x[0] for x in fields] + [x[0][0, 1] for x in mates])

    def add_part(spectra, p):
        at = jnp.bitwise_xor(group, jnp.where(core == 0, p, reverse(p)))
        return cross_spectra(
            jnp.stack([at, core]).astype(jnp.int32),
            blocks,
            groups,
            spectra,
            left,
            [parts[p] for parts in gathered],
            [parts[reverse(p)] for parts in mates],
        )

    spectra = add_part(None, 0)
    for step in range(bits):
        for parts in gathered:
            parts += [across(x, step) for x in parts]
    for parts, arrived in zip(mates, gathered):
        parts += [to_mate(x) for x in arrived[1:-1]]
    for p in range(1, groups - 1):
        spectra = add_part(spectra, p)
    spectra, lasts = lax.optimization_barrier((spectra, [parts[-1] for parts in gathered]))
    for c in range(CHUNKS):
        gathered[c][-1] = lasts[c]
        mates[c].append(to_mate(lasts[c]))
    spectra = add_part(spectra, groups - 1)
    return (spectra, field_pressure)


def solution(mesh):
    placed = (
        P(None, "node"),
        P(),
        P(),
        P("mode", "node"),
        P(None, "mode"),
        P(None, "mode", "node"),
    )
    return jax.shard_map(
        functools.partial(body, mesh.shape["node"], mesh.shape["mode"]),
        mesh=mesh,
        in_specs=placed,
        out_specs=(P(None, ("node", "mode"), None), P(("node", "mode"), None)),
        check_vma=False,
    )
```

```python
import functools

import jax
import jax.numpy as jnp
from jax import lax
from jax.experimental import pallas as pl
from jax.experimental.pallas import tpu as pltpu
from jax.sharding import PartitionSpec as P

SINE = (4.441535719696892, -7.264680836400963, 3.2520496076552887)
COSINE = (1.414204080330576, -6.977642043687199, 5.715238221214665, -1.7283481089755481)
COORD_PIECES = (0, 0, 1, 1, 0, 2)
WAVE_PIECES = (0, 1, 0, 1, 2, 0)
TURNS = 0.15915494309189535
CHUNKS = 2
ROWS, LANES, DIRECT = 32, 256, 1
BIG = pltpu.CompilerParams(vmem_limit_bytes=48 << 20)


def circle(turns):
    r = turns - jnp.round(turns)
    u = r * r
    s = r * (SINE[0] + u * (SINE[1] + u * SINE[2]))
    c = COSINE[0] + u * (COSINE[1] + u * (COSINE[2] + u * COSINE[3]))
    return c * c - 1.0, s * c


def pieces(x, order):
    first = x.astype(jnp.bfloat16).astype(jnp.float32)
    second = (x - first).astype(jnp.bfloat16).astype(jnp.float32)
    third = x - first - second
    blank = jnp.zeros((8 - x.shape[0], x.shape[1]), jnp.float32)
    parts = [jnp.concatenate([p, blank], axis=0) for p in (first, second, third)]
    return jnp.concatenate([parts[i] for i in order], axis=0).astype(jnp.bfloat16)


def forces_kernel(
    piece,
    coords_ref,
    wave_ref,
    shapes_ref,
    mine_ref,
    other_ref,
    spread,
    wave_pieces,
    even_turns,
    odd_turns,
    even,
    odd,
):
    step = pl.program_id(0)
    waves = wave_ref.shape[1]
    own = waves // 2
    count = shapes_ref.shape[1] // piece
    nodes = coords_ref.shape[1]
    turns, load = (even_turns, odd_turns), (even, odd)
    direct = DIRECT * LANES

    def phase(start, into):
        at = pl.multiple_of(start + direct, LANES)
        into[...] = jnp.dot(
            wave_pieces[...],
            pieces(coords_ref[:, pl.ds(at, piece - direct)], COORD_PIECES),
            preferred_element_type=jnp.float32,
        )

    def points(start, angles, into):
        for j in range(0, piece, LANES):
            columns = slice(j, j + LANES)
            if j < direct:
                at = pl.multiple_of(start + j, LANES)
                x, y, z = (coords_ref[i : i + 1, pl.ds(at, LANES)] for i in range(3))
            for w in range(0, waves, ROWS):
                rows = slice(w, w + ROWS)
                if j < direct:
                    a, b, c = (spread[i, rows, :] for i in range(3))
                    angle = a * x + b * y + c * z
                else:
                    angle = angles[rows, j - direct : j - direct + LANES]
                cosine, sine = circle(angle)
                to = w if w < own else w + own
                into[to : to + ROWS, columns] = cosine.astype(jnp.bfloat16)
                into[to + own : to + own + ROWS, columns] = sine.astype(jnp.bfloat16)

    @pl.when(step == 0)
    def _():
        first, second = wave_ref[:, :own], wave_ref[:, own:]
        swap = lax.rem(lax.axis_index("node"), 2) == 1
        ordered = TURNS * jnp.concatenate(
            [jnp.where(swap, second, first), jnp.where(swap, first, second)], axis=1
        )
        wave_pieces[...] = pieces(ordered, WAVE_PIECES).astype(jnp.float32).T.astype(jnp.bfloat16)
        columns = jnp.concatenate([ordered, jnp.zeros((5, waves), jnp.float32)], axis=0).T
        for i in range(3):
            spread[i] = jnp.broadcast_to(columns[:, i : i + 1], (waves, LANES))
        mine_ref[...] = jnp.zeros_like(mine_ref)
        other_ref[...] = jnp.zeros_like(other_ref)
        phase(0, turns[0])
        phase(piece, turns[1])
        points(0, turns[0], load[0])

    def wrapped(start):
        return jnp.where(start >= nodes, 0, start)

    for p in range(count):
        here = (step * count + p) * piece
        phase(wrapped(here + 2 * piece), turns[p % 2])
        points(wrapped(here + piece), turns[(p + 1) % 2], load[(p + 1) % 2])
        product = lax.dot_general(
            shapes_ref[:, p * piece : (p + 1) * piece],
            load[p % 2][...],
            (((1,), (1,)), ((), ())),
            preferred_element_type=jnp.float32,
        )
        mine_ref[...] += product[:, :waves]
        other_ref[...] += product[:, waves:]


def unit_forces(coords, wavevec, mode_shapes):
    modes, nodes = mode_shapes.shape
    waves = wavevec.shape[1]
    block, piece = 4096, 1024
    out = jax.ShapeDtypeStruct((modes, waves), jnp.float32)
    return pl.pallas_call(
        functools.partial(forces_kernel, piece),
        grid=(nodes // block,),
        in_specs=[
            pl.BlockSpec((3, nodes), lambda i: (0, 0)),
            pl.BlockSpec((3, waves), lambda i: (0, 0)),
            pl.BlockSpec((modes, block), lambda i: (0, i)),
        ],
        out_specs=[pl.BlockSpec((modes, waves), lambda i: (0, 0))] * 2,
        out_shape=[out, out],
        scratch_shapes=[
            pltpu.VMEM((3, waves, LANES), jnp.float32),
            pltpu.VMEM((waves, 8 * len(WAVE_PIECES)), jnp.bfloat16),
            pltpu.VMEM((waves, piece - DIRECT * LANES), jnp.float32),
            pltpu.VMEM((waves, piece - DIRECT * LANES), jnp.float32),
            pltpu.VMEM((2 * waves, piece), jnp.bfloat16),
            pltpu.VMEM((2 * waves, piece), jnp.bfloat16),
        ],
        compiler_params=pltpu.CompilerParams(vmem_limit_bytes=60 << 20),
        cost_estimate=pl.CostEstimate(
            flops=12 * modes * nodes * waves, bytes_accessed=2 * modes * nodes, transcendentals=0
        ),
    )(coords, wavevec, mode_shapes)


def field_kernel(
    blocks, kept_ref, last_ref, amp_ref, frf_ref, own_ref, mate_ref, *refs
):
    totals, sends, whole = refs[:CHUNKS], refs[CHUNKS:-1], refs[-1]
    forces = kept_ref[...] + last_ref[...].astype(jnp.float32)
    waves = forces.shape[1] // 2
    cosine, sine = forces[:, :waves], forces[:, waves:]
    swap = lax.rem(lax.axis_index("node"), 2) == 1
    amp = jnp.where(swap, amp_ref[:, waves:], amp_ref[:, :waves])
    amp_real, amp_imag = amp[0:1, :], amp[1:2, :]
    force_real = amp_real * cosine - amp_imag * sine
    force_imag = amp_real * sine + amp_imag * cosine
    frf = frf_ref[...].T
    gain_real, gain_imag = frf[:, 0:1], frf[:, 1:2]
    real = gain_real * force_real - gain_imag * force_imag
    imag = gain_real * force_imag + gain_imag * force_real
    upper = jnp.concatenate([real, imag], axis=1).astype(jnp.bfloat16)
    lower = jnp.concatenate([-imag, real], axis=1).astype(jnp.bfloat16)
    over_modes = (((0,), (0,)), ((), ()))
    width = own_ref.shape[2] // blocks
    size = waves // CHUNKS
    turned = width % 128 != 0
    for side, transfer in enumerate((own_ref, mate_ref)):
        whole[...] = lax.dot_general(
            upper, transfer[0], over_modes, preferred_element_type=jnp.float32
        ) + lax.dot_general(lower, transfer[1], over_modes, preferred_element_type=jnp.float32)
        for k in range(blocks):
            if turned:
                field = whole[:, k * width : (k + 1) * width]
            else:
                to = lax.rem(lax.axis_index("mode") + k, blocks)
                field = whole[:, pl.ds(pl.multiple_of(to * width, width), width)]
            for c in range(CHUNKS):
                part = jnp.concatenate(
                    [
                        field[c * size : (c + 1) * size],
                        field[waves + c * size : waves + (c + 1) * size],
                    ],
                    axis=0,
                )
                if k == 0:
                    totals[c][side] = part
                else:
                    sends[c * (blocks - 1) + k - 1][side] = part.astype(jnp.bfloat16)


def partial_fields(blocks, kept, last, amp, frf, own, mate):
    waves = kept.shape[1]
    width = own.shape[2] // blocks
    shape = (2, waves // CHUNKS, width)
    if width % 128 != 0:
        mode = lax.axis_index("mode")

        def turn(x):
            doubled = jnp.concatenate([x, x[:, :, : (blocks - 1) * width]], axis=2)
            return lax.dynamic_slice_in_dim(doubled, mode * width, blocks * width, 2)

        own, mate = turn(own), turn(mate)
    out = pl.pallas_call(
        functools.partial(field_kernel, blocks),
        out_shape=[jax.ShapeDtypeStruct(shape, jnp.float32)] * CHUNKS
        + [jax.ShapeDtypeStruct(shape, jnp.bfloat16)] * (CHUNKS * (blocks - 1)),
        scratch_shapes=[pltpu.VMEM((waves, own.shape[2]), jnp.float32)],
        compiler_params=BIG,
        cost_estimate=pl.CostEstimate(
            flops=8 * own.shape[1] * own.shape[2] * waves,
            bytes_accessed=4 * own.size,
            transcendentals=0,
        ),
    )(kept, last, amp, frf, own, mate)
    return out[:CHUNKS], [
        out[CHUNKS + c * (blocks - 1) : CHUNKS + (c + 1) * (blocks - 1)] for c in range(CHUNKS)
    ]


def own_rows_kernel(*refs):
    fields, left, pressure = refs[:-2], refs[-2], refs[-1]
    rows = left.shape[1] // 2
    size = left.shape[2] // 2
    waves = pressure.shape[1] // 2
    swap = lax.rem(lax.axis_index("node"), 2) == 1
    turned = [ref[...].astype(jnp.float32).T for ref in fields]
    for n, field in enumerate(turned):
        real, imag = field[:, :size], field[:, size:]
        left[n, :rows] = field.astype(jnp.bfloat16)
        left[n, rows:] = jnp.concatenate([imag, -real], axis=1).astype(jnp.bfloat16)
    real = [field[:, :size] for field in turned]
    imag = [field[:, size:] for field in turned]
    for part, at in ((real, 0), (imag, waves)):
        ours = jnp.concatenate(part[:CHUNKS], axis=1)
        theirs = jnp.concatenate(part[CHUNKS:], axis=1)
        half = slice(at, at + waves // 2), slice(at + waves // 2, at + waves)
        pressure[:, half[0]] = jnp.where(swap, theirs, ours).astype(jnp.bfloat16)
        pressure[:, half[1]] = jnp.where(swap, ours, theirs).astype(jnp.bfloat16)


def own_rows(fields):
    depth, rows = fields[0].shape
    return pl.pallas_call(
        own_rows_kernel,
        out_shape=[
            jax.ShapeDtypeStruct((len(fields), 2 * rows, depth), jnp.bfloat16),
            jax.ShapeDtypeStruct((rows, len(fields) * depth), jnp.bfloat16),
        ],
        compiler_params=BIG,
    )(*fields)


def spectra_kernel(blocks, place_ref, left_ref, *refs):
    data, out_ref = refs[: 2 * CHUNKS], refs[-1]
    depth, rows = data[0].shape[-2:]
    mode = lax.axis_index("mode")
    order = [lax.rem(mode - z + blocks, blocks) for z in range(blocks)]
    left = jnp.concatenate([left_ref[n] for n in range(len(data))], axis=1)
    for side in range(2):
        sides = [jnp.bitwise_xor(side, place_ref[1]), jnp.bitwise_xor(side, 1 - place_ref[1])]
        right = jnp.concatenate(
            [
                jnp.concatenate([ref[at, sides[n // CHUNKS]] for at in order], axis=1)
                for n, ref in enumerate(data)
            ],
            axis=0,
        )
        total = jnp.dot(left, right, preferred_element_type=jnp.float32) * (1.0 / (CHUNKS * depth))
        columns = slice(side * blocks * rows, (side + 1) * blocks * rows)
        out_ref[0, :, columns] = total[:rows]
        out_ref[1, :, columns] = total[rows:]


def cross_spectra(place, blocks, groups, spectra, left, ours, theirs):
    depth, rows = ours[0].shape[-2:]
    started = spectra is not None
    return pl.pallas_call(
        functools.partial(spectra_kernel, blocks),
        grid_spec=pltpu.PrefetchScalarGridSpec(
            num_scalar_prefetch=1,
            grid=(1,),
            in_specs=[pl.BlockSpec(left.shape, lambda s, place_ref: (0, 0, 0))]
            + [pl.BlockSpec(ours[0].shape, lambda s, place_ref: (0, 0, 0, 0))] * (2 * CHUNKS)
            + [pl.BlockSpec(memory_space=pl.ANY)] * started,
            out_specs=pl.BlockSpec(
                (2, rows, 2 * blocks * rows), lambda s, place_ref: (0, 0, place_ref[0])
            ),
        ),
        out_shape=jax.ShapeDtypeStruct((2, rows, 2 * groups * blocks * rows), jnp.float32),
        input_output_aliases={2 + 2 * CHUNKS: 0} if started else {},
        compiler_params=BIG,
        cost_estimate=pl.CostEstimate(
            flops=160 * CHUNKS * depth * rows * rows * blocks,
            bytes_accessed=32 * rows * rows * blocks,
            transcendentals=0,
        ),
    )(place, left, *ours, *theirs, *([spectra] if started else []))


def body(nodes, blocks, coords, wavevec, wave_amp, mode_shapes, modal_frf, radiation):
    groups = nodes // 2
    bits = groups.bit_length() - 1
    node = lax.axis_index("node")
    group, core = node // 2, lax.rem(node, 2)

    def reverse(p):
        return sum(((p >> b) & 1) << (bits - 1 - b) for b in range(bits))

    def to_mate(x):
        return lax.ppermute(x, "node", [(i, i ^ 1) for i in range(nodes)])

    def across(x, step):
        def flip(i):
            return i ^ (2 << (step if i % 2 == 0 else bits - 1 - step))

        return lax.ppermute(x, "node", [(i, flip(i)) for i in range(nodes)])

    def along(x, k):
        return lax.ppermute(x, "mode", [(i, (i + k) % blocks) for i in range(blocks)])

    far_first = sorted(range(1, blocks), key=lambda k: (-min(k, blocks - k), -k))
    mate = to_mate(radiation)
    mine, other = unit_forces(coords, wavevec, mode_shapes)
    kept = mine + to_mate(other)
    for step in range(bits - 1):
        kept = kept + across(kept.astype(jnp.bfloat16), step).astype(jnp.float32)
    last = across(kept.astype(jnp.bfloat16), bits - 1)
    totals, sends = partial_fields(blocks, kept, last, wave_amp, modal_frf, radiation, mate)

    fields = []
    for total, sent in zip(totals, sends):
        for k in far_first:
            total = total + along(sent[k - 1], k).astype(jnp.float32)
        fields.append(total.astype(jnp.bfloat16))
    gathered = []
    for field in fields:
        came = {k: along(field, k) for k in far_first}
        gathered.append([jnp.stack([field] + [came[k] for k in range(1, blocks)])])
    mates = [[to_mate(x) for x in parts] for parts in gathered]
    left, field_pressure = own_rows([x[0] for x in fields] + [x[0][0, 1] for x in mates])

    def add_part(spectra, p):
        at = jnp.bitwise_xor(group, jnp.where(core == 0, p, reverse(p)))
        return cross_spectra(
            jnp.stack([at, core]).astype(jnp.int32),
            blocks,
            groups,
            spectra,
            left,
            [parts[p] for parts in gathered],
            [parts[reverse(p)] for parts in mates],
        )

    spectra = add_part(None, 0)
    for step in range(bits):
        for parts in gathered:
            parts += [across(x, step) for x in parts]
    for parts, arrived in zip(mates, gathered):
        parts += [to_mate(x) for x in arrived[1:-1]]
    for p in range(1, groups - 1):
        spectra = add_part(spectra, p)
    spectra, lasts = lax.optimization_barrier((spectra, [parts[-1] for parts in gathered]))
    for c in range(CHUNKS):
        gathered[c][-1] = lasts[c]
        mates[c].append(to_mate(lasts[c]))
    spectra = add_part(spectra, groups - 1)
    return (spectra, field_pressure)


def solution(mesh):
    placed = (
        P(None, "node"),
        P(),
        P(),
        P("mode", "node"),
        P(None, "mode"),
        P(None, "mode", "node"),
    )
    return jax.shard_map(
        functools.partial(body, mesh.shape["node"], mesh.shape["mode"]),
        mesh=mesh,
        in_specs=placed,
        out_specs=(P(None, ("node", "mode"), None), P(("node", "mode"), None)),
        check_vma=False,
    )
```
